768 devices in a mesh: shot: 24 (over x_lo, z), gx: 4 (over x_hi, core), gy: 8 (over y).
Axes of the slice: x: 4 (x_hi: 2, x_lo: 2; x = x_hi * 2 + x_lo), y: 8, z: 12, core: 2. Of those that a mesh axis runs over, the one named last changes fastest.
Arguments:
- partials: float32 [24, 9, 24, 32, 1024], P('shot', None, None, 'gx', 'gy'), may hold values from -16 to 16, as said below
- hist_s: float32 [5, 3, 24, 32, 1024], P(None, None, 'shot', 'gx', 'gy'), may hold values from -30 to 30
- hist_y: float32 [5, 3, 24, 32, 1024], P(None, None, 'shot', 'gx', 'gy'), may hold values from -70 to 70, as said below
Outputs:
- direction: float32 [3, 24, 32, 1024], P(None, 'shot', 'gx', 'gy')
The draws below stay inside these ranges and needn't reach their ends.
Inputs may be any that keep to these rules, and one draw needn't show every extreme that they name: `partials`: for every shot group and cell, entries 3, 4, 5 are positive and each exceeds the sum of the magnitudes of the two off-diagonal entries of its row of the 3x3 matrix [[e3, e6, e7], [e6, e4, e8], [e7, e8, e5]]. Each entry of hist_y times the matching entry of hist_s is at least 0.2 times the square of that hist_s entry.
All inputs are finite; a program needn't handle non-finite values.
Results may differ from the reference program's by a relative error of at most 0.00013.
Values sent between devices are 32-bit elements; how exact they have to be, the bound alone decides.
A program may use at most 32 MiB of HBM per device.

```python
import jax
import jax.numpy as jnp
from jax import lax

PAIRS = 5
NX = 32
NY = 1024
NZ = 24
N_SHOT = 24


def common_field(key):
    return jax.random.truncated_normal(jax.random.fold_in(key, 101), -4.0, 4.0, (3, NZ, NX, NY), jnp.float32)


def log_uniform(key, shape, lowest, highest):
    return jnp.exp(jax.random.uniform(key, shape, jnp.float32, jnp.log(lowest), jnp.log(highest)))


def rise_field():
    depth = (jnp.arange(NZ, dtype=jnp.float32) / NZ)[:, None, None]
    across = (jnp.arange(NX, dtype=jnp.float32) / NX)[None, :, None]
    along = (jnp.arange(NY, dtype=jnp.float32) / NY)[None, None, :]
    return jnp.sqrt((1.0 + 2.0 * depth) * (1.0 + 2.0 * across) * (1.0 + 2.0 * along))


def draw_partials(key, part):
    shared = common_field(key)
    grad_scale = log_uniform(jax.random.fold_in(key, 102), (3, NZ, NX, NY), 0.5, 2.0)
    own_part = jax.random.truncated_normal(jax.random.fold_in(key, 103), -4.0, 4.0, (N_SHOT, 3, NZ, NX, NY), jnp.float32)
    gradients = (shared * grad_scale)[None] + 2.0 * own_part
    cell_scale = log_uniform(jax.random.fold_in(key, 104), (NZ, NX, NY), 0.5, 2.0)
    diagonal = jax.random.uniform(jax.random.fold_in(key, 105), (N_SHOT, 3, NZ, NX, NY), jnp.float32, 2.0, 4.0)
    offdiag = jax.random.uniform(jax.random.fold_in(key, 106), (N_SHOT, 3, NZ, NX, NY), jnp.float32, 0.2, 0.9)
    return jnp.concatenate([gradients, cell_scale * diagonal, cell_scale * offdiag], axis=1)


def history_pair(key):
    shared = common_field(key)
    own_part = jax.random.truncated_normal(jax.random.fold_in(key, 201), -4.0, 4.0, (PAIRS, 3, NZ, NX, NY), jnp.float32)
    updates = (0.6 * shared[None] + 0.8 * own_part) * rise_field()
    curvature = log_uniform(jax.random.fold_in(key, 202), (3, NZ, NX, NY), 0.5, 2.0)
    jitter = jax.random.uniform(jax.random.fold_in(key, 203), (PAIRS, 3, NZ, NX, NY), jnp.float32, -1.0, 1.0)
    changes = curvature * updates + 0.3 * jnp.abs(updates) * jitter
    return (updates, changes)


def draw_hist_s(key, part):
    return history_pair(key)[0]


def draw_hist_y(key, part):
    return history_pair(key)[1]


def setup_inputs(seed: int = 0) -> dict:
    key_list = jax.random.split(jax.random.key(seed), 4)
    partials = draw_partials(jax.random.fold_in(key_list[3], 71), 0)
    hist_s = draw_hist_s(jax.random.fold_in(key_list[3], 71), 0)
    hist_y = draw_hist_y(jax.random.fold_in(key_list[3], 71), 0)
    return dict(partials=partials, hist_s=hist_s, hist_y=hist_y)


def smooth_block(padded):
    along_x = 0.25 * (padded[:, :, :-2] + 2.0 * padded[:, :, 1:-1] + padded[:, :, 2:])
    return 0.25 * (along_x[..., :-2] + 2.0 * along_x[..., 1:-1] + along_x[..., 2:])


def apply_inverse(hessian, vectors):
    diag_p = hessian[0]
    diag_s = hessian[1]
    diag_r = hessian[2]
    cross_ps = hessian[3]
    cross_pr = hessian[4]
    cross_sr = hessian[5]
    cof_pp = diag_s * diag_r - cross_sr * cross_sr
    cof_ps = cross_pr * cross_sr - cross_ps * diag_r
    cof_pr = cross_ps * cross_sr - diag_s * cross_pr
    cof_ss = diag_p * diag_r - cross_pr * cross_pr
    cof_sr = cross_ps * cross_pr - diag_p * cross_sr
    cof_rr = diag_p * diag_s - cross_ps * cross_ps
    determinant = diag_p * cof_pp + cross_ps * cof_ps + cross_pr * cof_pr
    inverse_det = 1.0 / determinant
    comp_one = vectors[:, 0]
    comp_two = vectors[:, 1]
    comp_three = vectors[:, 2]
    return jnp.stack([
        (cof_pp * comp_one + cof_ps * comp_two + cof_pr * comp_three) * inverse_det,
        (cof_ps * comp_one + cof_ss * comp_two + cof_sr * comp_three) * inverse_det,
        (cof_pr * comp_one + cof_sr * comp_two + cof_rr * comp_three) * inverse_det], axis=1)


def pair_dots(left_flat, right_flat):
    return lax.dot_general(left_flat, right_flat, (((1,), (1,)), ((), ())),
                           precision=lax.Precision.HIGHEST, preferred_element_type=jnp.float32)


def upper_solve(matrix, values):
    count = matrix.shape[0]
    found = [None] * count
    for row in range(count - 1, -1, -1):
        total = values[row]
        for col in range(row + 1, count):
            total = total - matrix[row, col] * found[col]
        found[row] = total / matrix[row, row]
    return jnp.stack(found)


def upper_transpose_solve(matrix, values):
    count = matrix.shape[0]
    found = [None] * count
    for row in range(count):
        total = values[row]
        for col in range(row):
            total = total - matrix[col, row] * found[col]
        found[row] = total / matrix[row, row]
    return jnp.stack(found)


def combine_terms(cross_gram, curv_gram, hist_dot, pre_dot, solved, hist_s):
    middle_part = jnp.diag(jnp.diag(cross_gram)) + curv_gram
    coef_p = upper_solve(cross_gram, hist_dot)
    right_hand = jnp.dot(middle_part, coef_p, precision=lax.Precision.HIGHEST) - pre_dot
    coef_q = upper_transpose_solve(cross_gram, right_hand)
    update_s = jnp.tensordot(coef_q, hist_s, axes=1, precision=lax.Precision.HIGHEST)
    update_z = jnp.tensordot(coef_p, solved[1:], axes=1, precision=lax.Precision.HIGHEST)
    return -(solved[0] + update_s - update_z)


def reference(partials, hist_s, hist_y):
    fields = jnp.sum(partials, axis=0) * (1.0 / N_SHOT)
    padded = jnp.pad(fields, ((0, 0), (0, 0), (1, 1), (1, 1)))
    smoothed = smooth_block(padded)
    gradient = smoothed[0:3]
    solved = apply_inverse(smoothed[3:9], jnp.concatenate([gradient[None], hist_y], axis=0))
    s_flat = hist_s.reshape(PAIRS, -1)
    y_flat = hist_y.reshape(PAIRS, -1)
    z_flat = solved[1:].reshape(PAIRS, -1)
    cross_gram = pair_dots(s_flat, y_flat)
    curv_gram = pair_dots(y_flat, z_flat)
    hist_dot = pair_dots(s_flat, gradient.reshape(1, -1))[:, 0]
    pre_dot = pair_dots(y_flat, solved[0].reshape(1, -1))[:, 0]
    return combine_terms(cross_gram, curv_gram, hist_dot, pre_dot, solved, hist_s)
```

```python
import jax
import jax.numpy as jnp
from jax import lax
from jax.experimental import pallas as pl
from jax.experimental.pallas import tpu as pltpu
from jax.sharding import PartitionSpec as P

PAIRS = 5
FIELDS = 9
Z = 12
X = 2
SHOT = Z * X
GX = 4
GY = 8
MESH = pl.DeviceIdType.MESH
SPLIT = 5

ORDER = (6, 5, -5, 4, -4, 3, -3, 2, -2, 1, -1, 0)
LAST = {3: 0, -3: 1, 2: 2, -2: 3, 1: 4, -1: 5}

CROSS = 0
CURV = 32
HIST = 47
PRE = 52
SUMS = 64


def rows_of(terms):
    sub = lax.broadcasted_iota(jnp.int32, (8, 128), 0)
    out = jnp.zeros((8, 128), jnp.float32)
    for i, term in enumerate(terms):
        out = jnp.where(sub == i, jnp.sum(term, axis=0, keepdims=True), out)
    return jnp.broadcast_to(jnp.sum(out, axis=1, keepdims=True), (8, 128))


def row_of_sums(terms, first):
    sub = lax.broadcasted_iota(jnp.int32, (8, 128), 0)
    lane = lax.broadcasted_iota(jnp.int32, (8, 128), 1)
    total = jnp.zeros((8, 128), jnp.float32)
    for start in range(0, len(terms), 8):
        tile = rows_of(terms[start : start + 8])
        total = total + jnp.where(lane == sub + (first + start), tile, 0.0)
    return jnp.sum(total, axis=0, keepdims=True)


def dot_tile(left, right):
    return left[0] * right[0] + left[1] * right[1] + left[2] * right[2]


def kernel(
    partials, hist_s, hist_y, out,
    own, pair, stage, last, s_tile, y_tile,
    rows_out, rows_in, cols_out, cols_in,
    row_a, all_a, row_b, all_b, splat,
    local_sem, pair_send, pair_recv, stage_send, stage_recv, last_send, last_recv,
    halo_send, halo_recv, a_send, a_recv, b_send, b_recv,
):
    shot = lax.axis_index("shot")
    gx = lax.axis_index("gx")
    gy = lax.axis_index("gy")
    z = lax.rem(shot, Z)
    xb = lax.div(shot, Z)
    base = xb * Z
    other = (1 - xb) * Z

    def along_z(step):
        return {"shot": base + lax.rem(z + (step + Z), Z)}

    def shot_peer(dx, dz):
        side = other if dx else base
        return {"shot": side + lax.rem(z + dz, Z)}

    def tile_peer(dx, dy):
        return {"gx": lax.rem(gx + (dx + GX), GX), "gy": lax.rem(gy + (dy + GY), GY)}

    shot_steps = [(dx, dz) for dx in range(X) for dz in range(Z) if (dx, dz) != (0, 0)]
    tile_steps = [(dx, dy) for dx in range(GX) for dy in range(GY) if (dx, dy) != (0, 0)]

    local = [
        pltpu.make_async_copy(partials.at[0, :, pl.ds(base, Z)], own, local_sem.at[0]),
        pltpu.make_async_copy(hist_s.at[:, :, 0], s_tile, local_sem.at[1]),
        pltpu.make_async_copy(hist_y.at[:, :, 0], y_tile, local_sem.at[2]),
    ]
    for copy in local:
        copy.start()

    barrier = pltpu.get_barrier_semaphore()
    for dx, dz in shot_steps:
        pl.semaphore_signal(barrier, inc=1, device_id=shot_peer(dx, dz), device_id_type=MESH)
    for dx, dy in tile_steps:
        pl.semaphore_signal(barrier, inc=1, device_id=tile_peer(dx, dy), device_id_type=MESH)
    pl.semaphore_wait(barrier, len(shot_steps) + len(tile_steps))

    started = []

    def send(src, dst, send_sem, recv_sem, device):
        copy = pltpu.make_async_remote_copy(
            src_ref=src, dst_ref=dst, send_sem=send_sem, recv_sem=recv_sem, device_id=device, device_id_type=MESH
        )
        copy.start()
        started.append(copy)
        return copy

    level = [lax.rem(z + (Z - s), Z) for s in ORDER]
    pair_copy = []
    for k in range(Z):
        pair_copy.append(
            send(partials.at[0, :, other + level[k]], pair.at[k], pair_send.at[k], pair_recv.at[k], {"shot": other + z})
        )

    local[1].wait()
    local[2].wait()
    s_vec = [[s_tile[i, c] for c in range(3)] for i in range(PAIRS)]
    y_vec = [[y_tile[i, c] for c in range(3)] for i in range(PAIRS)]
    cross = [dot_tile(s_vec[i], y_vec[j]) for i in range(PAIRS) for j in range(PAIRS)]
    row_a[0:1] = row_of_sums(cross, CROSS)
    local[0].wait()

    slot = {s: k for k, s in enumerate(ORDER)}
    stage_copy = {}
    last_copy = {}
    for s in (6, 5, -5, 4, -4):
        k = slot[s]
        pair_copy[k].wait_recv()
        pair[k] = pair[k] + own[:, level[k]]
        if s == 6:
            stage_copy["r6"] = send(
                pair.at[k, 0:SPLIT], stage.at[2, 0:SPLIT], stage_send.at[2], stage_recv.at[2], along_z(-3)
            )
            stage_copy["l6"] = send(
                pair.at[k, SPLIT:FIELDS], stage.at[5, SPLIT:FIELDS], stage_send.at[5], stage_recv.at[5], along_z(3)
            )
        elif s > 0:
            stage_copy[s] = send(pair.at[k], stage.at[s - 4], stage_send.at[s - 4], stage_recv.at[s - 4], along_z(3 - s))
        else:
            stage_copy[s] = send(
                pair.at[k], stage.at[-s - 1], stage_send.at[-s - 1], stage_recv.at[-s - 1], along_z(-3 - s)
            )
    for s in (3, -3, 2, -2, 1, -1):
        k = slot[s]
        pair_copy[k].wait_recv()
        pair[k] = pair[k] + own[:, level[k]]
        if abs(s) < 3:
            m = LAST[s]
            last_copy[s] = send(pair.at[k], last.at[m], last_send.at[m], last_recv.at[m], along_z(-s))
    for s in (3, -3):
        k = slot[s]
        m = LAST[s]
        if s > 0:
            stage_copy["r6"].wait_recv()
            stage_copy[5].wait_recv()
            stage_copy[4].wait_recv()
            pair[k] = pair[k] + stage[0] + stage[1]
            pair[k, 0:SPLIT] = pair[k, 0:SPLIT] + stage[2, 0:SPLIT]
        else:
            stage_copy["l6"].wait_recv()
            stage_copy[-5].wait_recv()
            stage_copy[-4].wait_recv()
            pair[k] = pair[k] + stage[3] + stage[4]
            pair[k, SPLIT:FIELDS] = pair[k, SPLIT:FIELDS] + stage[5, SPLIT:FIELDS]
        last_copy[s] = send(pair.at[k], last.at[m], last_send.at[m], last_recv.at[m], along_z(-s))
    k = slot[0]
    pair_copy[k].wait_recv()
    mine = pair[k] + own[:, z]
    for s in (1, -1, 2, -2, 3, -3):
        last_copy[s].wait_recv()
        mine = mine + last[LAST[s]]
    mine = mine * (1.0 / SHOT)
    field = [mine[f] for f in range(FIELDS)]

    sub = lax.broadcasted_iota(jnp.int32, (8, 128), 0)
    lane = lax.broadcasted_iota(jnp.int32, (8, 128), 1)
    columns = jnp.zeros((8, 128), jnp.float32)
    for f in range(FIELDS):
        rows_out[0, f : f + 1] = field[f][0:1]
        rows_out[1, f : f + 1] = field[f][7:8]
        columns = jnp.where(lane == f, field[f] if f == 0 else pltpu.roll(field[f], f, 1), columns)
        columns = jnp.where(lane == 16 + f, pltpu.roll(field[f], 17 + f, 1), columns)
    cols_out[...] = columns
    halo = []
    for n, (dx, dy) in enumerate(((-1, -1), (1, -1), (-1, 1), (1, 1), (0, -1), (0, 1))):
        halo.append(send(cols_out, cols_in.at[n], halo_send.at[n], halo_recv.at[n], tile_peer(dx, dy)))
    halo.append(send(rows_out.at[0, 0:FIELDS], rows_in.at[0, 0:FIELDS], halo_send.at[6], halo_recv.at[6], tile_peer(-1, 0)))
    halo.append(send(rows_out.at[1, 0:FIELDS], rows_in.at[1, 0:FIELDS], halo_send.at[7], halo_recv.at[7], tile_peer(1, 0)))
    for copy in halo:
        copy.wait_recv()
    has_up, has_down = gx > 0, gx < GX - 1
    has_left, has_right = gy > 0, gy < GY - 1

    def along_x(center, above, below):
        up = jnp.where(sub == 0, jnp.where(has_up, above, 0.0), pltpu.roll(center, 1, 0))
        down = jnp.where(sub == 7, jnp.where(has_down, below, 0.0), pltpu.roll(center, 7, 0))
        return 0.25 * (up + 2.0 * center + down)

    def wide(row):
        return jnp.broadcast_to(row, (8, 128))

    left = along_x(cols_in[5], wide(cols_in[3, 7:8]), wide(cols_in[2, 0:1]))
    right = along_x(cols_in[4], wide(cols_in[1, 7:8]), wide(cols_in[0, 0:1]))
    left = jnp.where(has_left, left, 0.0)
    right = jnp.where(has_right, right, 0.0)
    smooth = []
    for f in range(FIELDS):
        mid = along_x(field[f], wide(rows_in[1, f : f + 1]), wide(rows_in[0, f : f + 1]))
        before = jnp.where(lane == 0, pltpu.roll(left, 112 - f, 1), pltpu.roll(mid, 1, 1))
        after = jnp.where(lane == 127, pltpu.roll(right, 127 - f, 1), pltpu.roll(mid, 127, 1))
        smooth.append(0.25 * (before + 2.0 * mid + after))

    gradient = smooth[0:3]
    diag_p, diag_s, diag_r, cross_ps, cross_pr, cross_sr = smooth[3:9]
    cof_pp = diag_s * diag_r - cross_sr * cross_sr
    cof_ps = cross_pr * cross_sr - cross_ps * diag_r
    cof_pr = cross_ps * cross_sr - diag_s * cross_pr
    cof_ss = diag_p * diag_r - cross_pr * cross_pr
    cof_sr = cross_ps * cross_pr - diag_p * cross_sr
    cof_rr = diag_p * diag_s - cross_ps * cross_ps
    inverse_det = 1.0 / (diag_p * cof_pp + cross_ps * cof_ps + cross_pr * cof_pr)

    def solve(v):
        return [
            (cof_pp * v[0] + cof_ps * v[1] + cof_pr * v[2]) * inverse_det,
            (cof_ps * v[0] + cof_ss * v[1] + cof_sr * v[2]) * inverse_det,
            (cof_pr * v[0] + cof_sr * v[1] + cof_rr * v[2]) * inverse_det,
        ]

    first = solve(gradient)
    solved = [solve(y_vec[i]) for i in range(PAIRS)]
    upper = [(i, j) for i in range(PAIRS) for j in range(i, PAIRS)]
    terms = [dot_tile(y_vec[i], solved[j]) for i, j in upper]
    terms += [dot_tile(s_vec[i], gradient) for i in range(PAIRS)]
    terms += [dot_tile(y_vec[i], first) for i in range(PAIRS)]
    row = row_a[0:1] + row_of_sums(terms, CURV)

    row_a[0:1] = row
    all_a[0:1] = row
    for n, (dx, dz) in enumerate(shot_steps):
        send(row_a.at[0:1], all_a.at[n + 1 : n + 2], a_send, a_recv, shot_peer(dx, dz))
        started.pop()
    rest_a = all_a.at[1:SHOT]
    pltpu.make_async_copy(rest_a, rest_a, a_recv).wait()
    row = jnp.sum(all_a[...], axis=0, keepdims=True)
    row_b[0:1] = row
    all_b[0:1] = row
    for n, (dx, dy) in enumerate(tile_steps):
        send(row_b.at[0:1], all_b.at[n + 1 : n + 2], b_send, b_recv, tile_peer(dx, dy))
        started.pop()
    rest_b = all_b.at[1 : GX * GY]
    pltpu.make_async_copy(rest_b, rest_b, b_recv).wait()
    row = jnp.sum(all_b[...], axis=0, keepdims=True)

    tall_row = lax.broadcasted_iota(jnp.int32, (SUMS, 128), 0)
    tall_lane = lax.broadcasted_iota(jnp.int32, (SUMS, 128), 1)
    picked = jnp.where(tall_row == tall_lane, jnp.broadcast_to(row, (SUMS, 128)), 0.0)
    splat[...] = jnp.broadcast_to(jnp.sum(picked, axis=1, keepdims=True), (SUMS, 128))

    def total(n):
        return splat[n : n + 1]

    cross_gram = [[total(CROSS + i * PAIRS + j) for j in range(PAIRS)] for i in range(PAIRS)]
    curv_gram = [[None] * PAIRS for _ in range(PAIRS)]
    for n, (i, j) in enumerate(upper):
        curv_gram[i][j] = curv_gram[j][i] = total(CURV + n)
    coef_p = [None] * PAIRS
    for i in range(PAIRS - 1, -1, -1):
        value = total(HIST + i)
        for j in range(i + 1, PAIRS):
            value = value - cross_gram[i][j] * coef_p[j]
        coef_p[i] = value / cross_gram[i][i]
    coef_q = [None] * PAIRS
    for i in range(PAIRS):
        value = cross_gram[i][i] * coef_p[i] - total(PRE + i)
        for j in range(PAIRS):
            value = value + curv_gram[i][j] * coef_p[j]
        for j in range(i):
            value = value - cross_gram[j][i] * coef_q[j]
        coef_q[i] = value / cross_gram[i][i]
    for c in range(3):
        value = first[c]
        for i in range(PAIRS):
            value = value + wide(coef_q[i]) * s_vec[i][c] - wide(coef_p[i]) * solved[i][c]
        out[c, 0] = -value

    for copy in started:
        copy.wait_send()
    pltpu.make_async_copy(rest_a, rest_a, a_send).wait()
    pltpu.make_async_copy(rest_b, rest_b, b_send).wait()


def per_device(partials, hist_s, hist_y):
    dma = pltpu.SemaphoreType.DMA
    f32 = jnp.float32
    chunk = (FIELDS, 8, 128)
    return pl.pallas_call(
        kernel,
        out_shape=jax.ShapeDtypeStruct((3, 1, 8, 128), f32),
        in_specs=[pl.BlockSpec(memory_space=pl.ANY)] * 3,
        out_specs=pl.BlockSpec(memory_space=pltpu.VMEM),
        scratch_shapes=[
            pltpu.VMEM((FIELDS, Z, 8, 128), f32),
            pltpu.VMEM((Z, *chunk), f32),
            pltpu.VMEM((6, *chunk), f32),
            pltpu.VMEM((6, *chunk), f32),
            pltpu.VMEM((PAIRS, 3, 8, 128), f32),
            pltpu.VMEM((PAIRS, 3, 8, 128), f32),
            pltpu.VMEM((2, 16, 128), f32),
            pltpu.VMEM((2, 16, 128), f32),
            pltpu.VMEM((8, 128), f32),
            pltpu.VMEM((6, 8, 128), f32),
            pltpu.VMEM((8, 128), f32),
            pltpu.VMEM((SHOT, 128), f32),
            pltpu.VMEM((8, 128), f32),
            pltpu.VMEM((GX * GY, 128), f32),
            pltpu.VMEM((SUMS, 128), f32),
            dma((3,)),
            dma((Z,)), dma((Z,)),
            dma((6,)), dma((6,)),
            dma((6,)), dma((6,)),
            dma((8,)), dma((8,)),
            dma, dma, dma, dma,
        ],
        compiler_params=pltpu.CompilerParams(collective_id=0, has_side_effects=True),
        name="lbfgs_direction",
    )(partials, hist_s, hist_y)


def solution(mesh):
    return jax.shard_map(
        per_device,
        mesh=mesh,
        in_specs=(
            P("shot", None, None, "gx", "gy"),
            P(None, None, "shot", "gx", "gy"),
            P(None, None, "shot", "gx", "gy"),
        ),
        out_specs=P(None, "shot", "gx", "gy"),
        check_vma=False,
    )
```

```python
import jax
import jax.numpy as jnp
from jax import lax
from jax.experimental import pallas as pl
from jax.experimental.pallas import tpu as pltpu
from jax.sharding import PartitionSpec as P

PAIRS = 5
FIELDS = 9
Z = 12
X = 2
SHOT = Z * X
GX = 4
GY = 8
MESH = pl.DeviceIdType.MESH
SPLIT = 5

ORDER = (6, 5, -5, 4, -4, 3, -3, 2, -2, 1, -1, 0)
STEPS = (1, 2, 3, -1, -2, -3)
LAST = {3: 0, -3: 1, 2: 2, -2: 3, 1: 4, -1: 5}

CROSS = 0
CURV = 32
HIST = 47
PRE = 52
SUMS = 64


def rows_of(terms):
    sub = lax.broadcasted_iota(jnp.int32, (8, 128), 0)
    out = jnp.zeros((8, 128), jnp.float32)
    for i, term in enumerate(terms):
        out = jnp.where(sub == i, jnp.sum(term, axis=0, keepdims=True), out)
    return jnp.broadcast_to(jnp.sum(out, axis=1, keepdims=True), (8, 128))


def row_of_sums(terms, first):
    sub = lax.broadcasted_iota(jnp.int32, (8, 128), 0)
    lane = lax.broadcasted_iota(jnp.int32, (8, 128), 1)
    total = jnp.zeros((8, 128), jnp.float32)
    for start in range(0, len(terms), 8):
        tile = rows_of(terms[start : start + 8])
        total = total + jnp.where(lane == sub + (first + start), tile, 0.0)
    return jnp.sum(total, axis=0, keepdims=True)


def dot_tile(left, right):
    return left[0] * right[0] + left[1] * right[1] + left[2] * right[2]


def kernel(
    partials, hist_s, hist_y, out,
    own, pair, stage, last, s_tile, y_tile,
    rows_out, rows_in, cols_out, cols_in,
    row_a, all_a, row_b, all_b, splat,
    local_sem, pair_send, pair_recv, stage_send, stage_recv, last_send, last_recv,
    halo_send, halo_recv, a_send, a_recv, b_send, b_recv, ready, known,
):
    shot = lax.axis_index("shot")
    gx = lax.axis_index("gx")
    gy = lax.axis_index("gy")
    z = lax.rem(shot, Z)
    xb = lax.div(shot, Z)
    base = xb * Z
    other = (1 - xb) * Z

    def along_z(step):
        return {"shot": base + lax.rem(z + (step + Z), Z)}

    def shot_peer(dx, dz):
        side = other if dx else base
        return {"shot": side + lax.rem(z + dz, Z)}

    def tile_peer(dx, dy):
        return {"gx": lax.rem(gx + (dx + GX), GX), "gy": lax.rem(gy + (dy + GY), GY)}

    shot_steps = [(dx, dz) for dx in range(X) for dz in range(Z) if (dx, dz) != (0, 0)]
    shot_steps.sort(key=lambda d: -(d[0] + min(d[1], Z - d[1])))
    tile_steps = [(dx, dy) for dx in range(GX) for dy in range(GY) if (dx, dy) != (0, 0)]
    tile_steps.sort(key=lambda d: -(min(d[0], 2) + min(d[1], GY - d[1])))

    local = [
        pltpu.make_async_copy(partials.at[0, :, pl.ds(base, Z)], own, local_sem.at[0]),
        pltpu.make_async_copy(hist_s.at[:, :, 0], s_tile, local_sem.at[1]),
        pltpu.make_async_copy(hist_y.at[:, :, 0], y_tile, local_sem.at[2]),
    ]
    for copy in local:
        copy.start()

    def plane(step):
        return lax.rem(z + (step + Z), Z)

    flip = lax.rem(gx + 2, GX)
    mate = gx + 1 - 2 * lax.rem(gx, 2)
    beside = (
        {"shot": other + z},
        {"shot": other + z, "gx": flip},
        {"gx": mate},
        tile_peer(0, 1),
        tile_peer(0, -1),
    )
    barrier = pltpu.get_barrier_semaphore()

    def signal(sem, device):
        pl.semaphore_signal(sem, inc=1, device_id=device, device_id_type=MESH)

    for device in beside:
        signal(barrier, device)
    lower = 0
    for step in STEPS:

        @pl.when(plane(step) > z)
        def _(step=step):
            signal(barrier, along_z(step))

        lower = lower + jnp.where(plane(step) < z, 1, 0)
    pl.semaphore_wait(barrier, len(beside) + lower)
    for step in STEPS:

        @pl.when(plane(step) < z)
        def _(step=step):
            signal(ready.at[STEPS.index(-step)], along_z(step))

    def await_plane(step):
        @pl.when(plane(step) > z)
        def _():
            pl.semaphore_wait(ready.at[STEPS.index(step)], 1)

    signal(known.at[0], {"shot": other + z})

    started = []

    def send(src, dst, send_sem, recv_sem, device):
        copy = pltpu.make_async_remote_copy(
            src_ref=src, dst_ref=dst, send_sem=send_sem, recv_sem=recv_sem, device_id=device, device_id_type=MESH
        )
        copy.start()
        started.append(copy)
        return copy

    level = [lax.rem(z + (Z - s), Z) for s in ORDER]
    pair_copy = []
    for k in range(Z):
        pair_copy.append(
            send(partials.at[0, :, other + level[k]], pair.at[k], pair_send.at[k], pair_recv.at[k], {"shot": other + z})
        )

    local[1].wait()
    local[2].wait()
    s_vec = [[s_tile[i, c] for c in range(3)] for i in range(PAIRS)]
    y_vec = [[y_tile[i, c] for c in range(3)] for i in range(PAIRS)]
    cross = [dot_tile(s_vec[i], y_vec[j]) for i in range(PAIRS) for j in range(PAIRS)]
    row_a[0:1] = row_of_sums(cross, CROSS)
    local[0].wait()

    pl.semaphore_wait(known.at[0], 1)
    signal(known.at[1], {"gx": mate})
    pl.semaphore_wait(known.at[1], 1)

    def pass_on(distance):
        if distance > 1:
            pl.semaphore_wait(known.at[2 * distance - 2], 1)
            pl.semaphore_wait(known.at[2 * distance - 1], 1)
        if distance <= GY // 2:
            signal(known.at[2 * distance], tile_peer(0, 1))
            signal(known.at[2 * distance + 1], tile_peer(0, -1))

    pass_on(1)

    slot = {s: k for k, s in enumerate(ORDER)}
    stage_copy = {}
    last_copy = {}
    for s in (6, 5, -5, 4, -4):
        k = slot[s]
        pair_copy[k].wait_recv()
        pair[k] = pair[k] + own[:, level[k]]
        if s == 6:
            await_plane(-3)
            await_plane(3)
            stage_copy["r6"] = send(
                pair.at[k, 0:SPLIT], stage.at[2, 0:SPLIT], stage_send.at[2], stage_recv.at[2], along_z(-3)
            )
            stage_copy["l6"] = send(
                pair.at[k, SPLIT:FIELDS], stage.at[5, SPLIT:FIELDS], stage_send.at[5], stage_recv.at[5], along_z(3)
            )
        elif s > 0:
            await_plane(3 - s)
            stage_copy[s] = send(pair.at[k], stage.at[s - 4], stage_send.at[s - 4], stage_recv.at[s - 4], along_z(3 - s))
        else:
            await_plane(-3 - s)
            stage_copy[s] = send(
                pair.at[k], stage.at[-s - 1], stage_send.at[-s - 1], stage_recv.at[-s - 1], along_z(-3 - s)
            )
    pass_on(2)
    for s in (3, -3, 2, -2, 1, -1):
        if s == -3:
            pass_on(3)
        if s == -2:
            pass_on(4)
        k = slot[s]
        pair_copy[k].wait_recv()
        pair[k] = pair[k] + own[:, level[k]]
        if abs(s) < 3:
            m = LAST[s]
            last_copy[s] = send(pair.at[k], last.at[m], last_send.at[m], last_recv.at[m], along_z(-s))
    for s in (3, -3):
        k = slot[s]
        m = LAST[s]
        if s > 0:
            stage_copy["r6"].wait_recv()
            stage_copy[5].wait_recv()
            stage_copy[4].wait_recv()
            pair[k] = pair[k] + stage[0] + stage[1]
            pair[k, 0:SPLIT] = pair[k, 0:SPLIT] + stage[2, 0:SPLIT]
        else:
            stage_copy["l6"].wait_recv()
            stage_copy[-5].wait_recv()
            stage_copy[-4].wait_recv()
            pair[k] = pair[k] + stage[3] + stage[4]
            pair[k, SPLIT:FIELDS] = pair[k, SPLIT:FIELDS] + stage[5, SPLIT:FIELDS]
        last_copy[s] = send(pair.at[k], last.at[m], last_send.at[m], last_recv.at[m], along_z(-s))
    pass_on(5)
    k = slot[0]
    pair_copy[k].wait_recv()
    mine = pair[k] + own[:, z]
    for s in (1, -1, 2, -2, 3, -3):
        last_copy[s].wait_recv()
        mine = mine + last[LAST[s]]
    mine = mine * (1.0 / SHOT)
    field = [mine[f] for f in range(FIELDS)]

    sub = lax.broadcasted_iota(jnp.int32, (8, 128), 0)
    lane = lax.broadcasted_iota(jnp.int32, (8, 128), 1)
    columns = jnp.zeros((8, 128), jnp.float32)
    for f in range(FIELDS):
        rows_out[0, f : f + 1] = field[f][0:1]
        rows_out[1, f : f + 1] = field[f][7:8]
        columns = jnp.where(lane == f, field[f] if f == 0 else pltpu.roll(field[f], f, 1), columns)
        columns = jnp.where(lane == 16 + f, pltpu.roll(field[f], 17 + f, 1), columns)
    cols_out[...] = columns
    halo = []
    for n, (dx, dy) in enumerate(((-1, -1), (1, -1), (-1, 1), (1, 1), (0, -1), (0, 1))):
        halo.append(send(cols_out, cols_in.at[n], halo_send.at[n], halo_recv.at[n], tile_peer(dx, dy)))
    halo.append(send(rows_out.at[0, 0:FIELDS], rows_in.at[0, 0:FIELDS], halo_send.at[6], halo_recv.at[6], tile_peer(-1, 0)))
    halo.append(send(rows_out.at[1, 0:FIELDS], rows_in.at[1, 0:FIELDS], halo_send.at[7], halo_recv.at[7], tile_peer(1, 0)))
    for copy in halo:
        copy.wait_recv()
    has_up, has_down = gx > 0, gx < GX - 1
    has_left, has_right = gy > 0, gy < GY - 1

    def along_x(center, above, below):
        up = jnp.where(sub == 0, jnp.where(has_up, above, 0.0), pltpu.roll(center, 1, 0))
        down = jnp.where(sub == 7, jnp.where(has_down, below, 0.0), pltpu.roll(center, 7, 0))
        return 0.25 * (up + 2.0 * center + down)

    def wide(row):
        return jnp.broadcast_to(row, (8, 128))

    left = along_x(cols_in[5], wide(cols_in[3, 7:8]), wide(cols_in[2, 0:1]))
    right = along_x(cols_in[4], wide(cols_in[1, 7:8]), wide(cols_in[0, 0:1]))
    left = jnp.where(has_left, left, 0.0)
    right = jnp.where(has_right, right, 0.0)
    smooth = []
    for f in range(FIELDS):
        mid = along_x(field[f], wide(rows_in[1, f : f + 1]), wide(rows_in[0, f : f + 1]))
        before = jnp.where(lane == 0, pltpu.roll(left, 112 - f, 1), pltpu.roll(mid, 1, 1))
        after = jnp.where(lane == 127, pltpu.roll(right, 127 - f, 1), pltpu.roll(mid, 127, 1))
        smooth.append(0.25 * (before + 2.0 * mid + after))

    gradient = smooth[0:3]
    diag_p, diag_s, diag_r, cross_ps, cross_pr, cross_sr = smooth[3:9]
    cof_pp = diag_s * diag_r - cross_sr * cross_sr
    cof_ps = cross_pr * cross_sr - cross_ps * diag_r
    cof_pr = cross_ps * cross_sr - diag_s * cross_pr
    cof_ss = diag_p * diag_r - cross_pr * cross_pr
    cof_sr = cross_ps * cross_pr - diag_p * cross_sr
    cof_rr = diag_p * diag_s - cross_ps * cross_ps
    inverse_det = 1.0 / (diag_p * cof_pp + cross_ps * cof_ps + cross_pr * cof_pr)

    def solve(v):
        return [
            (cof_pp * v[0] + cof_ps * v[1] + cof_pr * v[2]) * inverse_det,
            (cof_ps * v[0] + cof_ss * v[1] + cof_sr * v[2]) * inverse_det,
            (cof_pr * v[0] + cof_sr * v[1] + cof_rr * v[2]) * inverse_det,
        ]

    first = solve(gradient)
    solved = [solve(y_vec[i]) for i in range(PAIRS)]
    upper = [(i, j) for i in range(PAIRS) for j in range(i, PAIRS)]
    terms = [dot_tile(y_vec[i], solved[j]) for i, j in upper]
    terms += [dot_tile(s_vec[i], gradient) for i in range(PAIRS)]
    terms += [dot_tile(y_vec[i], first) for i in range(PAIRS)]
    row = row_a[0:1] + row_of_sums(terms, CURV)

    row_a[0:1] = row
    all_a[0:1] = row
    for n, (dx, dz) in enumerate(shot_steps):
        send(row_a.at[0:1], all_a.at[n + 1 : n + 2], a_send, a_recv, shot_peer(dx, dz))
        started.pop()
    rest_a = all_a.at[1:SHOT]
    pltpu.make_async_copy(rest_a, rest_a, a_recv).wait()
    row = jnp.sum(all_a[...], axis=0, keepdims=True)
    row_b[0:1] = row
    all_b[0:1] = row
    for n, (dx, dy) in enumerate(tile_steps):
        send(row_b.at[0:1], all_b.at[n + 1 : n + 2], b_send, b_recv, tile_peer(dx, dy))
        started.pop()
    rest_b = all_b.at[1 : GX * GY]
    pltpu.make_async_copy(rest_b, rest_b, b_recv).wait()
    row = jnp.sum(all_b[...], axis=0, keepdims=True)

    tall_row = lax.broadcasted_iota(jnp.int32, (SUMS, 128), 0)
    tall_lane = lax.broadcasted_iota(jnp.int32, (SUMS, 128), 1)
    picked = jnp.where(tall_row == tall_lane, jnp.broadcast_to(row, (SUMS, 128)), 0.0)
    splat[...] = jnp.broadcast_to(jnp.sum(picked, axis=1, keepdims=True), (SUMS, 128))

    def total(n):
        return splat[n : n + 1]

    cross_gram = [[total(CROSS + i * PAIRS + j) for j in range(PAIRS)] for i in range(PAIRS)]
    curv_gram = [[None] * PAIRS for _ in range(PAIRS)]
    for n, (i, j) in enumerate(upper):
        curv_gram[i][j] = curv_gram[j][i] = total(CURV + n)
    coef_p = [None] * PAIRS
    for i in range(PAIRS - 1, -1, -1):
        value = total(HIST + i)
        for j in range(i + 1, PAIRS):
            value = value - cross_gram[i][j] * coef_p[j]
        coef_p[i] = value / cross_gram[i][i]
    coef_q = [None] * PAIRS
    for i in range(PAIRS):
        value = cross_gram[i][i] * coef_p[i] - total(PRE + i)
        for j in range(PAIRS):
            value = value + curv_gram[i][j] * coef_p[j]
        for j in range(i):
            value = value - cross_gram[j][i] * coef_q[j]
        coef_q[i] = value / cross_gram[i][i]
    for c in range(3):
        value = first[c]
        for i in range(PAIRS):
            value = value + wide(coef_q[i]) * s_vec[i][c] - wide(coef_p[i]) * solved[i][c]
        out[c, 0] = -value

    for copy in started:
        copy.wait_send()
    pltpu.make_async_copy(rest_a, rest_a, a_send).wait()
    pltpu.make_async_copy(rest_b, rest_b, b_send).wait()


def per_device(partials, hist_s, hist_y):
    dma = pltpu.SemaphoreType.DMA
    f32 = jnp.float32
    chunk = (FIELDS, 8, 128)
    return pl.pallas_call(
        kernel,
        out_shape=jax.ShapeDtypeStruct((3, 1, 8, 128), f32),
        in_specs=[pl.BlockSpec(memory_space=pltpu.HBM)] * 3,
        out_specs=pl.BlockSpec(memory_space=pltpu.VMEM),
        scratch_shapes=[
            pltpu.VMEM((FIELDS, Z, 8, 128), f32),
            pltpu.VMEM((Z, *chunk), f32),
            pltpu.VMEM((6, *chunk), f32),
            pltpu.VMEM((6, *chunk), f32),
            pltpu.VMEM((PAIRS, 3, 8, 128), f32),
            pltpu.VMEM((PAIRS, 3, 8, 128), f32),
            pltpu.VMEM((2, 16, 128), f32),
            pltpu.VMEM((2, 16, 128), f32),
            pltpu.VMEM((8, 128), f32),
            pltpu.VMEM((6, 8, 128), f32),
            pltpu.VMEM((8, 128), f32),
            pltpu.VMEM((SHOT, 128), f32),
            pltpu.VMEM((8, 128), f32),
            pltpu.VMEM((GX * GY, 128), f32),
            pltpu.VMEM((SUMS, 128), f32),
            dma((3,)),
            dma((Z,)), dma((Z,)),
            dma((6,)), dma((6,)),
            dma((6,)), dma((6,)),
            dma((8,)), dma((8,)),
            dma, dma, dma, dma,
            pltpu.SemaphoreType.REGULAR((len(STEPS),)),
            pltpu.SemaphoreType.REGULAR((2 + GY,)),
        ],
        compiler_params=pltpu.CompilerParams(collective_id=0, has_side_effects=True, vmem_limit_bytes=56_512_000),
        name="lbfgs_direction",
    )(partials, hist_s, hist_y)


def solution(mesh):
    return jax.shard_map(
        per_device,
        mesh=mesh,
        in_specs=(
            P("shot", None, None, "gx", "gy"),
            P(None, None, "shot", "gx", "gy"),
            P(None, None, "shot", "gx", "gy"),
        ),
        out_specs=P(None, "shot", "gx", "gy"),
        check_vma=False,
    )
```

```python
import jax
import jax.numpy as jnp
from jax import lax
from jax.experimental import pallas as pl
from jax.experimental.pallas import tpu as pltpu
from jax.sharding import PartitionSpec as P

PAIRS = 5
FIELDS = 9
Z = 12
X = 2
SHOT = Z * X
GX = 4
GY = 8
MESH = pl.DeviceIdType.MESH
SPLIT = 5

ORDER = (6, 5, -5, 4, -4, 3, -3, 2, -2, 1, -1, 0)
STEPS = (1, 2, 3, -1, -2, -3)
LAST = {3: 0, -3: 1, 2: 2, -2: 3, 1: 4, -1: 5}

CROSS = 0
CURV = 32
HIST = 47
PRE = 52
SUMS = 64


def rows_of(terms):
    sub = lax.broadcasted_iota(jnp.int32, (8, 128), 0)
    out = jnp.zeros((8, 128), jnp.float32)
    for i, term in enumerate(terms):
        out = jnp.where(sub == i, jnp.sum(term, axis=0, keepdims=True), out)
    return jnp.broadcast_to(jnp.sum(out, axis=1, keepdims=True), (8, 128))


def row_of_sums(terms, first):
    sub = lax.broadcasted_iota(jnp.int32, (8, 128), 0)
    lane = lax.broadcasted_iota(jnp.int32, (8, 128), 1)
    total = jnp.zeros((8, 128), jnp.float32)
    for start in range(0, len(terms), 8):
        tile = rows_of(terms[start : start + 8])
        total = total + jnp.where(lane == sub + (first + start), tile, 0.0)
    return jnp.sum(total, axis=0, keepdims=True)


def dot_tile(left, right):
    return left[0] * right[0] + left[1] * right[1] + left[2] * right[2]


def kernel(
    partials, hist_s, hist_y, out,
    own, pair, stage, last, s_tile, y_tile,
    rows_out, rows_in, cols_out, cols_in,
    row_a, all_a, row_b, all_b, splat,
    local_sem, pair_send, pair_recv, stage_send, stage_recv, last_send, last_recv,
    halo_send, halo_recv, a_send, a_recv, b_send, b_recv, ready, known,
):
    shot = lax.axis_index("shot")
    gx = lax.axis_index("gx")
    gy = lax.axis_index("gy")
    z = lax.rem(shot, Z)
    xb = lax.div(shot, Z)
    base = xb * Z
    other = (1 - xb) * Z

    def along_z(step):
        return {"shot": base + lax.rem(z + (step + Z), Z)}

    def shot_peer(dx, dz):
        side = other if dx else base
        return {"shot": side + lax.rem(z + dz, Z)}

    def tile_peer(dx, dy):
        return {"gx": lax.rem(gx + (dx + GX), GX), "gy": lax.rem(gy + (dy + GY), GY)}

    shot_steps = [(dx, dz) for dx in range(X) for dz in range(Z) if (dx, dz) != (0, 0)]
    shot_steps.sort(key=lambda d: -(d[0] + min(d[1], Z - d[1])))
    tile_steps = [(dx, dy) for dx in range(GX) for dy in range(GY) if (dx, dy) != (0, 0)]
    tile_steps.sort(key=lambda d: -(min(d[0], 2) + min(d[1], GY - d[1])))

    local = [
        pltpu.make_async_copy(partials.at[0], own, local_sem.at[0]),
        pltpu.make_async_copy(hist_s.at[:, :, 0], s_tile, local_sem.at[1]),
        pltpu.make_async_copy(hist_y.at[:, :, 0], y_tile, local_sem.at[2]),
    ]
    for copy in local:
        copy.start()

    def plane(step):
        return lax.rem(z + (step + Z), Z)

    half = GY // 2
    ring = jnp.where(gy > half, GY - gy, gy)
    flip = {"gx": lax.rem(gx + 2, GX)}
    mate = {"gx": gx + 1 - 2 * lax.rem(gx, 2)}
    outer = [(tile_peer(0, 1), gy < half), (tile_peer(0, -1), (gy == 0) | (gy > half))]
    inner = [(tile_peer(0, -1), (gy > 0) & (gy <= half)), (tile_peer(0, 1), gy >= half)]
    barrier = pltpu.get_barrier_semaphore()

    def signal(sem, device):
        pl.semaphore_signal(sem, inc=1, device_id=device, device_id_type=MESH)

    def signal_if(wanted, sem, device):
        @pl.when(wanted)
        def _():
            signal(sem, device)

    signal(barrier, {"shot": other + z})
    signal(barrier, mate)
    expected = 2 + jnp.where(gx >= 2, 1, 0) + jnp.where(gy == half, 2, jnp.where(gy == 0, 0, 1))
    for device, wanted in outer:
        signal_if(wanted, barrier, device)
    signal_if(gx < 2, barrier, flip)
    for step in STEPS:
        signal_if(plane(step) > z, barrier, along_z(step))
        expected = expected + jnp.where(plane(step) < z, 1, 0)
    pl.semaphore_wait(barrier, expected)

    def tell_earlier():
        for step in STEPS:
            signal_if(plane(step) < z, ready.at[STEPS.index(-step)], along_z(step))
        signal_if(gx >= 2, known.at[0], flip)

    def await_plane(step):
        @pl.when(plane(step) > z)
        def _():
            pl.semaphore_wait(ready.at[STEPS.index(step)], 1)

    def know_row():
        @pl.when(gx < 2)
        def _():
            pl.semaphore_wait(known.at[0], 1)

        signal(known.at[1], mate)
        pl.semaphore_wait(known.at[1], 1)

        @pl.when(ring == half)
        def _():
            for device, _ in inner:
                signal(known.at[2], device)

    def know_outer(distance):
        @pl.when(ring == distance)
        def _():
            pl.semaphore_wait(known.at[2], 1 if distance else 2)
            if distance:
                for device, wanted in inner:
                    signal_if(wanted, known.at[2], device)
            else:
                for device, _ in outer:
                    signal(known.at[3], device)

    def know_all():
        @pl.when(ring > 0)
        def _():
            pl.semaphore_wait(known.at[3], jnp.where(ring == half, 2, 1))

            @pl.when(ring < half)
            def _():
                for device, wanted in outer:
                    signal_if(wanted, known.at[3], device)

    started = []

    def send(src, dst, send_sem, recv_sem, device):
        copy = pltpu.make_async_remote_copy(
            src_ref=src, dst_ref=dst, send_sem=send_sem, recv_sem=recv_sem, device_id=device, device_id_type=MESH
        )
        copy.start()
        started.append(copy)
        return copy

    local[0].wait()
    level = [lax.rem(z + (Z - s), Z) for s in ORDER]
    pair_copy = []
    for k in range(Z):
        pair_copy.append(
            send(own.at[:, other + level[k]], pair.at[k], pair_send.at[k], pair_recv.at[k], {"shot": other + z})
        )

    tell_earlier()
    local[1].wait()
    local[2].wait()
    s_vec = [[s_tile[i, c] for c in range(3)] for i in range(PAIRS)]
    y_vec = [[y_tile[i, c] for c in range(3)] for i in range(PAIRS)]
    cross = [dot_tile(s_vec[i], y_vec[j]) for i in range(PAIRS) for j in range(PAIRS)]
    row_a[0:1] = row_of_sums(cross, CROSS)

    know_row()
    slot = {s: k for k, s in enumerate(ORDER)}
    stage_copy = {}
    last_copy = {}
    for s in (6, 5, -5, 4, -4):
        k = slot[s]
        pair_copy[k].wait_recv()
        pair[k] = pair[k] + own[:, base + level[k]]
        if s == 5:
            know_outer(3)
        if s == 4:
            know_outer(2)
        if s == 6:
            await_plane(-3)
            await_plane(3)
            stage_copy["r6"] = send(
                pair.at[k, 0:SPLIT], stage.at[2, 0:SPLIT], stage_send.at[2], stage_recv.at[2], along_z(-3)
            )
            stage_copy["l6"] = send(
                pair.at[k, SPLIT:FIELDS], stage.at[5, SPLIT:FIELDS], stage_send.at[5], stage_recv.at[5], along_z(3)
            )
        elif s > 0:
            await_plane(3 - s)
            stage_copy[s] = send(pair.at[k], stage.at[s - 4], stage_send.at[s - 4], stage_recv.at[s - 4], along_z(3 - s))
        else:
            await_plane(-3 - s)
            stage_copy[s] = send(
                pair.at[k], stage.at[-s - 1], stage_send.at[-s - 1], stage_recv.at[-s - 1], along_z(-3 - s)
            )
    def add_own(s):
        k = slot[s]
        pair_copy[k].wait_recv()
        pair[k] = pair[k] + own[:, base + level[k]]

    def send_last(s):
        m = LAST[s]
        last_copy[s] = send(pair.at[slot[s]], last.at[m], last_send.at[m], last_recv.at[m], along_z(-s))

    def gather(s):
        k = slot[s]
        if s > 0:
            first_slot, low, high, far = 0, 0, SPLIT, "r6"
        else:
            first_slot, low, high, far = 3, SPLIT, FIELDS, "l6"
        add_own(s)
        for key in (far, s + s // 3 * 2, s + s // 3):
            stage_copy[key].wait_recv()
        pair[k] = pair[k] + stage[first_slot] + stage[first_slot + 1]
        pair[k, low:high] = pair[k, low:high] + stage[first_slot + 2, low:high]
        send_last(s)

    add_own(2)
    send_last(2)
    know_outer(1)
    add_own(-2)
    send_last(-2)
    gather(3)
    gather(-3)
    know_outer(0)
    add_own(1)
    send_last(1)
    add_own(-1)
    send_last(-1)
    know_all()
    k = slot[0]
    pair_copy[k].wait_recv()
    mine = pair[k] + own[:, shot]
    for s in (1, -1, 2, -2, 3, -3):
        last_copy[s].wait_recv()
        mine = mine + last[LAST[s]]
    mine = mine * (1.0 / SHOT)
    field = [mine[f] for f in range(FIELDS)]

    sub = lax.broadcasted_iota(jnp.int32, (8, 128), 0)
    lane = lax.broadcasted_iota(jnp.int32, (8, 128), 1)
    columns = jnp.zeros((8, 128), jnp.float32)
    for f in range(FIELDS):
        rows_out[0, f : f + 1] = field[f][0:1]
        rows_out[1, f : f + 1] = field[f][7:8]
        columns = jnp.where(lane == f, field[f] if f == 0 else pltpu.roll(field[f], f, 1), columns)
        columns = jnp.where(lane == 16 + f, pltpu.roll(field[f], 17 + f, 1), columns)
    cols_out[...] = columns
    halo = []
    for n, (dx, dy) in enumerate(((-1, -1), (1, -1), (-1, 1), (1, 1), (0, -1), (0, 1))):
        halo.append(send(cols_out, cols_in.at[n], halo_send.at[n], halo_recv.at[n], tile_peer(dx, dy)))
    halo.append(send(rows_out.at[0, 0:FIELDS], rows_in.at[0, 0:FIELDS], halo_send.at[6], halo_recv.at[6], tile_peer(-1, 0)))
    halo.append(send(rows_out.at[1, 0:FIELDS], rows_in.at[1, 0:FIELDS], halo_send.at[7], halo_recv.at[7], tile_peer(1, 0)))
    for copy in halo:
        copy.wait_recv()
    has_up, has_down = gx > 0, gx < GX - 1
    has_left, has_right = gy > 0, gy < GY - 1

    def along_x(center, above, below):
        up = jnp.where(sub == 0, jnp.where(has_up, above, 0.0), pltpu.roll(center, 1, 0))
        down = jnp.where(sub == 7, jnp.where(has_down, below, 0.0), pltpu.roll(center, 7, 0))
        return 0.25 * (up + 2.0 * center + down)

    def wide(row):
        return jnp.broadcast_to(row, (8, 128))

    left = along_x(cols_in[5], wide(cols_in[3, 7:8]), wide(cols_in[2, 0:1]))
    right = along_x(cols_in[4], wide(cols_in[1, 7:8]), wide(cols_in[0, 0:1]))
    left = jnp.where(has_left, left, 0.0)
    right = jnp.where(has_right, right, 0.0)
    smooth = []
    for f in range(FIELDS):
        mid = along_x(field[f], wide(rows_in[1, f : f + 1]), wide(rows_in[0, f : f + 1]))
        before = jnp.where(lane == 0, pltpu.roll(left, 112 - f, 1), pltpu.roll(mid, 1, 1))
        after = jnp.where(lane == 127, pltpu.roll(right, 127 - f, 1), pltpu.roll(mid, 127, 1))
        smooth.append(0.25 * (before + 2.0 * mid + after))

    gradient = smooth[0:3]
    diag_p, diag_s, diag_r, cross_ps, cross_pr, cross_sr = smooth[3:9]
    cof_pp = diag_s * diag_r - cross_sr * cross_sr
    cof_ps = cross_pr * cross_sr - cross_ps * diag_r
    cof_pr = cross_ps * cross_sr - diag_s * cross_pr
    cof_ss = diag_p * diag_r - cross_pr * cross_pr
    cof_sr = cross_ps * cross_pr - diag_p * cross_sr
    cof_rr = diag_p * diag_s - cross_ps * cross_ps
    inverse_det = 1.0 / (diag_p * cof_pp + cross_ps * cof_ps + cross_pr * cof_pr)

    def solve(v):
        return [
            (cof_pp * v[0] + cof_ps * v[1] + cof_pr * v[2]) * inverse_det,
            (cof_ps * v[0] + cof_ss * v[1] + cof_sr * v[2]) * inverse_det,
            (cof_pr * v[0] + cof_sr * v[1] + cof_rr * v[2]) * inverse_det,
        ]

    first = solve(gradient)
    solved = [solve(y_vec[i]) for i in range(PAIRS)]
    upper = [(i, j) for i in range(PAIRS) for j in range(i, PAIRS)]
    terms = [dot_tile(y_vec[i], solved[j]) for i, j in upper]
    terms += [dot_tile(s_vec[i], gradient) for i in range(PAIRS)]
    terms += [dot_tile(y_vec[i], first) for i in range(PAIRS)]
    row = row_a[0:1] + row_of_sums(terms, CURV)

    row_a[0:1] = row
    all_a[0:1] = row
    for n, (dx, dz) in enumerate(shot_steps):
        send(row_a.at[0:1], all_a.at[n + 1 : n + 2], a_send, a_recv, shot_peer(dx, dz))
        started.pop()
    rest_a = all_a.at[1:SHOT]
    pltpu.make_async_copy(rest_a, rest_a, a_recv).wait()
    row = jnp.sum(all_a[...], axis=0, keepdims=True)
    row_b[0:1] = row
    all_b[0:1] = row
    for n, (dx, dy) in enumerate(tile_steps):
        send(row_b.at[0:1], all_b.at[n + 1 : n + 2], b_send, b_recv, tile_peer(dx, dy))
        started.pop()
    rest_b = all_b.at[1 : GX * GY]
    pltpu.make_async_copy(rest_b, rest_b, b_recv).wait()
    row = jnp.sum(all_b[...], axis=0, keepdims=True)

    tall_row = lax.broadcasted_iota(jnp.int32, (SUMS, 128), 0)
    tall_lane = lax.broadcasted_iota(jnp.int32, (SUMS, 128), 1)
    picked = jnp.where(tall_row == tall_lane, jnp.broadcast_to(row, (SUMS, 128)), 0.0)
    splat[...] = jnp.broadcast_to(jnp.sum(picked, axis=1, keepdims=True), (SUMS, 128))

    def total(n):
        return splat[n : n + 1]

    cross_gram = [[total(CROSS + i * PAIRS + j) for j in range(PAIRS)] for i in range(PAIRS)]
    curv_gram = [[None] * PAIRS for _ in range(PAIRS)]
    for n, (i, j) in enumerate(upper):
        curv_gram[i][j] = curv_gram[j][i] = total(CURV + n)
    coef_p = [None] * PAIRS
    for i in range(PAIRS - 1, -1, -1):
        value = total(HIST + i)
        for j in range(i + 1, PAIRS):
            value = value - cross_gram[i][j] * coef_p[j]
        coef_p[i] = value / cross_gram[i][i]
    coef_q = [None] * PAIRS
    for i in range(PAIRS):
        value = cross_gram[i][i] * coef_p[i] - total(PRE + i)
        for j in range(PAIRS):
            value = value + curv_gram[i][j] * coef_p[j]
        for j in range(i):
            value = value - cross_gram[j][i] * coef_q[j]
        coef_q[i] = value / cross_gram[i][i]
    for c in range(3):
        value = first[c]
        for i in range(PAIRS):
            value = value + wide(coef_q[i]) * s_vec[i][c] - wide(coef_p[i]) * solved[i][c]
        out[c, 0] = -value

    for copy in started:
        copy.wait_send()
    pltpu.make_async_copy(rest_a, rest_a, a_send).wait()
    pltpu.make_async_copy(rest_b, rest_b, b_send).wait()


def per_device(partials, hist_s, hist_y):
    dma = pltpu.SemaphoreType.DMA
    f32 = jnp.float32
    chunk = (FIELDS, 8, 128)
    return pl.pallas_call(
        kernel,
        out_shape=jax.ShapeDtypeStruct((3, 1, 8, 128), f32),
        in_specs=[pl.BlockSpec(memory_space=pltpu.HBM)] * 3,
        out_specs=pl.BlockSpec(memory_space=pltpu.VMEM),
        scratch_shapes=[
            pltpu.VMEM((FIELDS, SHOT, 8, 128), f32),
            pltpu.VMEM((Z, *chunk), f32),
            pltpu.VMEM((6, *chunk), f32),
            pltpu.VMEM((6, *chunk), f32),
            pltpu.VMEM((PAIRS, 3, 8, 128), f32),
            pltpu.VMEM((PAIRS, 3, 8, 128), f32),
            pltpu.VMEM((2, 16, 128), f32),
            pltpu.VMEM((2, 16, 128), f32),
            pltpu.VMEM((8, 128), f32),
            pltpu.VMEM((6, 8, 128), f32),
            pltpu.VMEM((8, 128), f32),
            pltpu.VMEM((SHOT, 128), f32),
            pltpu.VMEM((8, 128), f32),
            pltpu.VMEM((GX * GY, 128), f32),
            pltpu.VMEM((SUMS, 128), f32),
            dma((3,)),
            dma((Z,)), dma((Z,)),
            dma((6,)), dma((6,)),
            dma((6,)), dma((6,)),
            dma((8,)), dma((8,)),
            dma, dma, dma, dma,
            pltpu.SemaphoreType.REGULAR((len(STEPS),)),
            pltpu.SemaphoreType.REGULAR((4,)),
        ],
        compiler_params=pltpu.CompilerParams(collective_id=0, has_side_effects=True, vmem_limit_bytes=56_512_000),
        name="lbfgs_direction",
    )(partials, hist_s, hist_y)


def solution(mesh):
    return jax.shard_map(
        per_device,
        mesh=mesh,
        in_specs=(
            P("shot", None, None, "gx", "gy"),
            P(None, None, "shot", "gx", "gy"),
            P(None, None, "shot", "gx", "gy"),
        ),
        out_specs=P(None, "shot", "gx", "gy"),
        check_vma=False,
    )
```

```python
import jax
import jax.numpy as jnp
from jax import lax
from jax.experimental import pallas as pl
from jax.experimental.pallas import tpu as pltpu
from jax.sharding import PartitionSpec as P

PAIRS = 5
FIELDS = 9
Z = 12
X = 2
SHOT = Z * X
GX = 4
GY = 8
MESH = pl.DeviceIdType.MESH
SPLIT = 5

ORDER = (6, 5, -5, 4, -4, 3, -3, 2, -2, 1, -1, 0)
STEPS = (1, 2, 3, -1, -2, -3)
LAST = {3: 0, -3: 1, 2: 2, -2: 3, 1: 4, -1: 5}

CROSS = 0
CURV = 32
HIST = 47
PRE = 52
SUMS = 64


def rows_of(terms):
    sub = lax.broadcasted_iota(jnp.int32, (8, 128), 0)
    out = jnp.zeros((8, 128), jnp.float32)
    for i, term in enumerate(terms):
        out = jnp.where(sub == i, jnp.sum(term, axis=0, keepdims=True), out)
    return jnp.broadcast_to(jnp.sum(out, axis=1, keepdims=True), (8, 128))


def row_of_sums(terms, first):
    sub = lax.broadcasted_iota(jnp.int32, (8, 128), 0)
    lane = lax.broadcasted_iota(jnp.int32, (8, 128), 1)
    total = jnp.zeros((8, 128), jnp.float32)
    for start in range(0, len(terms), 8):
        tile = rows_of(terms[start : start + 8])
        total = total + jnp.where(lane == sub + (first + start), tile, 0.0)
    return jnp.sum(total, axis=0, keepdims=True)


def dot_tile(left, right):
    return left[0] * right[0] + left[1] * right[1] + left[2] * right[2]


def kernel(
    partials, hist_s, hist_y, out,
    own, pair, stage, last, s_tile, y_tile,
    rows_out, rows_in, cols_out, cols_in,
    row_a, all_a, row_b, all_b, splat,
    local_sem, pair_send, pair_recv, stage_send, stage_recv, last_send, last_recv,
    halo_send, halo_recv, a_send, a_recv, b_send, b_recv, ready, known,
):
    shot = lax.axis_index("shot")
    gx = lax.axis_index("gx")
    gy = lax.axis_index("gy")
    z = lax.rem(shot, Z)
    xb = lax.div(shot, Z)
    base = xb * Z
    other = (1 - xb) * Z

    def along_z(step):
        return {"shot": base + lax.rem(z + (step + Z), Z)}

    def tile_peer(dx, dy):
        return {"gx": lax.rem(gx + (dx + GX), GX), "gy": lax.rem(gy + (dy + GY), GY)}

    far = lambda step, count: min(step, count - step)
    z_steps = sorted(range(1, Z), key=lambda dz: -far(dz, Z))
    plane_steps = [(dl, dx, dy) for dl in range(X) for dx in range(GX) for dy in range(GY)][1:]
    plane_steps.sort(key=lambda d: -(d[0] + far(d[1], GX) + far(d[2], GY)))

    def plane_peer(dl, dx, dy):
        return {"shot": (other if dl else base) + z} | tile_peer(dx, dy)

    local = [
        pltpu.make_async_copy(partials.at[0], own, local_sem.at[0]),
        pltpu.make_async_copy(hist_s.at[:, :, 0], s_tile, local_sem.at[1]),
        pltpu.make_async_copy(hist_y.at[:, :, 0], y_tile, local_sem.at[2]),
    ]
    for copy in local:
        copy.start()

    def plane(step):
        return lax.rem(z + (step + Z), Z)

    half = GY // 2
    ring = jnp.where(gy > half, GY - gy, gy)
    flip = {"gx": lax.rem(gx + 2, GX)}
    mate = {"gx": gx + 1 - 2 * lax.rem(gx, 2)}
    outer = [(tile_peer(0, 1), gy < half), (tile_peer(0, -1), (gy == 0) | (gy > half))]
    inner = [(tile_peer(0, -1), (gy > 0) & (gy <= half)), (tile_peer(0, 1), gy >= half)]
    barrier = pltpu.get_barrier_semaphore()

    def signal(sem, device):
        pl.semaphore_signal(sem, inc=1, device_id=device, device_id_type=MESH)

    def signal_if(wanted, sem, device):
        @pl.when(wanted)
        def _():
            signal(sem, device)

    signal(barrier, {"shot": other + z})
    signal(barrier, mate)
    expected = 2 + jnp.where(gx >= 2, 1, 0) + jnp.where(gy == half, 2, jnp.where(gy == 0, 0, 1))
    for device, wanted in outer:
        signal_if(wanted, barrier, device)
    signal_if(gx < 2, barrier, flip)
    for step in STEPS:
        signal_if(plane(step) > z, barrier, along_z(step))
        expected = expected + jnp.where(plane(step) < z, 1, 0)
    pl.semaphore_wait(barrier, expected)

    def tell_earlier():
        for step in STEPS:
            signal_if(plane(step) < z, ready.at[STEPS.index(-step)], along_z(step))
        signal_if(gx >= 2, known.at[0], flip)

    def await_plane(step):
        @pl.when(plane(step) > z)
        def _():
            pl.semaphore_wait(ready.at[STEPS.index(step)], 1)

    def know_row():
        @pl.when(gx < 2)
        def _():
            pl.semaphore_wait(known.at[0], 1)

        signal(known.at[1], mate)
        pl.semaphore_wait(known.at[1], 1)

        @pl.when(ring == half)
        def _():
            for device, _ in inner:
                signal(known.at[2], device)

    def know_outer(distance):
        @pl.when(ring == distance)
        def _():
            pl.semaphore_wait(known.at[2], 1 if distance else 2)
            if distance:
                for device, wanted in inner:
                    signal_if(wanted, known.at[2], device)
            else:
                for device, _ in outer:
                    signal(known.at[3], device)

    def know_all():
        @pl.when(ring > 0)
        def _():
            pl.semaphore_wait(known.at[3], jnp.where(ring == half, 2, 1))

            @pl.when(ring < half)
            def _():
                for device, wanted in outer:
                    signal_if(wanted, known.at[3], device)

    started = []

    def send(src, dst, send_sem, recv_sem, device):
        copy = pltpu.make_async_remote_copy(
            src_ref=src, dst_ref=dst, send_sem=send_sem, recv_sem=recv_sem, device_id=device, device_id_type=MESH
        )
        copy.start()
        started.append(copy)
        return copy

    local[0].wait()
    level = [lax.rem(z + (Z - s), Z) for s in ORDER]
    pair_copy = []
    for k in range(Z):
        pair_copy.append(
            send(own.at[:, other + level[k]], pair.at[k], pair_send.at[k], pair_recv.at[k], {"shot": other + z})
        )

    tell_earlier()
    local[1].wait()
    local[2].wait()
    s_vec = [[s_tile[i, c] for c in range(3)] for i in range(PAIRS)]
    y_vec = [[y_tile[i, c] for c in range(3)] for i in range(PAIRS)]
    cross = [dot_tile(s_vec[i], y_vec[j]) for i in range(PAIRS) for j in range(PAIRS)]
    row_a[0:1] = row_of_sums(cross, CROSS)

    know_row()
    slot = {s: k for k, s in enumerate(ORDER)}
    stage_copy = {}
    last_copy = {}
    for s in (6, 5, -5, 4, -4):
        k = slot[s]
        pair_copy[k].wait_recv()
        pair[k] = pair[k] + own[:, base + level[k]]
        if s == 5:
            know_outer(3)
        if s == 4:
            know_outer(2)
        if s == 6:
            await_plane(-3)
            await_plane(3)
            stage_copy["r6"] = send(
                pair.at[k, 0:SPLIT], stage.at[2, 0:SPLIT], stage_send.at[2], stage_recv.at[2], along_z(-3)
            )
            stage_copy["l6"] = send(
                pair.at[k, SPLIT:FIELDS], stage.at[5, SPLIT:FIELDS], stage_send.at[5], stage_recv.at[5], along_z(3)
            )
        elif s > 0:
            await_plane(3 - s)
            stage_copy[s] = send(pair.at[k], stage.at[s - 4], stage_send.at[s - 4], stage_recv.at[s - 4], along_z(3 - s))
        else:
            await_plane(-3 - s)
            stage_copy[s] = send(
                pair.at[k], stage.at[-s - 1], stage_send.at[-s - 1], stage_recv.at[-s - 1], along_z(-3 - s)
            )
    def add_own(s):
        k = slot[s]
        pair_copy[k].wait_recv()
        pair[k] = pair[k] + own[:, base + level[k]]

    def send_last(s):
        m = LAST[s]
        last_copy[s] = send(pair.at[slot[s]], last.at[m], last_send.at[m], last_recv.at[m], along_z(-s))

    def gather(s):
        k = slot[s]
        if s > 0:
            first_slot, low, high, far = 0, 0, SPLIT, "r6"
        else:
            first_slot, low, high, far = 3, SPLIT, FIELDS, "l6"
        add_own(s)
        for key in (far, s + s // 3 * 2, s + s // 3):
            stage_copy[key].wait_recv()
        pair[k] = pair[k] + stage[first_slot] + stage[first_slot + 1]
        pair[k, low:high] = pair[k, low:high] + stage[first_slot + 2, low:high]
        send_last(s)

    add_own(2)
    send_last(2)
    know_outer(1)
    add_own(-2)
    send_last(-2)
    gather(3)
    gather(-3)
    know_outer(0)
    add_own(1)
    send_last(1)
    add_own(-1)
    send_last(-1)
    know_all()
    k = slot[0]
    pair_copy[k].wait_recv()
    mine = pair[k] + own[:, shot]
    for s in (1, -1, 2, -2, 3, -3):
        last_copy[s].wait_recv()
        mine = mine + last[LAST[s]]
    mine = mine * (1.0 / SHOT)
    field = [mine[f] for f in range(FIELDS)]

    sub = lax.broadcasted_iota(jnp.int32, (8, 128), 0)
    lane = lax.broadcasted_iota(jnp.int32, (8, 128), 1)
    columns = jnp.zeros((8, 128), jnp.float32)
    for f in range(FIELDS):
        rows_out[0, f : f + 1] = field[f][0:1]
        rows_out[1, f : f + 1] = field[f][7:8]
        columns = jnp.where(lane == f, field[f] if f == 0 else pltpu.roll(field[f], f, 1), columns)
        columns = jnp.where(lane == 16 + f, pltpu.roll(field[f], 17 + f, 1), columns)
    cols_out[...] = columns
    halo = []
    for n, (dx, dy) in enumerate(((-1, -1), (1, -1), (-1, 1), (1, 1), (0, -1), (0, 1))):
        halo.append(send(cols_out, cols_in.at[n], halo_send.at[n], halo_recv.at[n], tile_peer(dx, dy)))
    halo.append(send(rows_out.at[0, 0:FIELDS], rows_in.at[0, 0:FIELDS], halo_send.at[6], halo_recv.at[6], tile_peer(-1, 0)))
    halo.append(send(rows_out.at[1, 0:FIELDS], rows_in.at[1, 0:FIELDS], halo_send.at[7], halo_recv.at[7], tile_peer(1, 0)))
    for copy in halo:
        copy.wait_recv()
    has_up, has_down = gx > 0, gx < GX - 1
    has_left, has_right = gy > 0, gy < GY - 1

    def along_x(center, above, below):
        up = jnp.where(sub == 0, jnp.where(has_up, above, 0.0), pltpu.roll(center, 1, 0))
        down = jnp.where(sub == 7, jnp.where(has_down, below, 0.0), pltpu.roll(center, 7, 0))
        return 0.25 * (up + 2.0 * center + down)

    def wide(row):
        return jnp.broadcast_to(row, (8, 128))

    left = along_x(cols_in[5], wide(cols_in[3, 7:8]), wide(cols_in[2, 0:1]))
    right = along_x(cols_in[4], wide(cols_in[1, 7:8]), wide(cols_in[0, 0:1]))
    left = jnp.where(has_left, left, 0.0)
    right = jnp.where(has_right, right, 0.0)
    smooth = []
    for f in range(FIELDS):
        mid = along_x(field[f], wide(rows_in[1, f : f + 1]), wide(rows_in[0, f : f + 1]))
        before = jnp.where(lane == 0, pltpu.roll(left, 112 - f, 1), pltpu.roll(mid, 1, 1))
        after = jnp.where(lane == 127, pltpu.roll(right, 127 - f, 1), pltpu.roll(mid, 127, 1))
        smooth.append(0.25 * (before + 2.0 * mid + after))

    gradient = smooth[0:3]
    diag_p, diag_s, diag_r, cross_ps, cross_pr, cross_sr = smooth[3:9]
    cof_pp = diag_s * diag_r - cross_sr * cross_sr
    cof_ps = cross_pr * cross_sr - cross_ps * diag_r
    cof_pr = cross_ps * cross_sr - diag_s * cross_pr
    cof_ss = diag_p * diag_r - cross_pr * cross_pr
    cof_sr = cross_ps * cross_pr - diag_p * cross_sr
    cof_rr = diag_p * diag_s - cross_ps * cross_ps
    inverse_det = 1.0 / (diag_p * cof_pp + cross_ps * cof_ps + cross_pr * cof_pr)

    def solve(v):
        return [
            (cof_pp * v[0] + cof_ps * v[1] + cof_pr * v[2]) * inverse_det,
            (cof_ps * v[0] + cof_ss * v[1] + cof_sr * v[2]) * inverse_det,
            (cof_pr * v[0] + cof_sr * v[1] + cof_rr * v[2]) * inverse_det,
        ]

    first = solve(gradient)
    solved = [solve(y_vec[i]) for i in range(PAIRS)]
    upper = [(i, j) for i in range(PAIRS) for j in range(i, PAIRS)]
    terms = [dot_tile(y_vec[i], solved[j]) for i, j in upper]
    terms += [dot_tile(s_vec[i], gradient) for i in range(PAIRS)]
    terms += [dot_tile(y_vec[i], first) for i in range(PAIRS)]
    row = row_a[0:1] + row_of_sums(terms, CURV)

    row_a[0:1] = row
    all_a[0:1] = row
    for n, dz in enumerate(z_steps):
        send(row_a.at[0:1], all_a.at[n + 1 : n + 2], a_send, a_recv, along_z(dz))
        started.pop()
    rest_a = all_a.at[1:Z]
    pltpu.make_async_copy(rest_a, rest_a, a_recv).wait()
    row = jnp.sum(all_a[...], axis=0, keepdims=True)
    row_b[0:1] = row
    all_b[0:1] = row
    for n, d in enumerate(plane_steps):
        send(row_b.at[0:1], all_b.at[n + 1 : n + 2], b_send, b_recv, plane_peer(*d))
        started.pop()
    rest_b = all_b.at[1 : X * GX * GY]
    pltpu.make_async_copy(rest_b, rest_b, b_recv).wait()
    row = jnp.sum(all_b[...], axis=0, keepdims=True)

    tall_row = lax.broadcasted_iota(jnp.int32, (SUMS, 128), 0)
    tall_lane = lax.broadcasted_iota(jnp.int32, (SUMS, 128), 1)
    picked = jnp.where(tall_row == tall_lane, jnp.broadcast_to(row, (SUMS, 128)), 0.0)
    splat[...] = jnp.broadcast_to(jnp.sum(picked, axis=1, keepdims=True), (SUMS, 128))

    def total(n):
        return splat[n : n + 1]

    cross_gram = [[total(CROSS + i * PAIRS + j) for j in range(PAIRS)] for i in range(PAIRS)]
    curv_gram = [[None] * PAIRS for _ in range(PAIRS)]
    for n, (i, j) in enumerate(upper):
        curv_gram[i][j] = curv_gram[j][i] = total(CURV + n)
    coef_p = [None] * PAIRS
    for i in range(PAIRS - 1, -1, -1):
        value = total(HIST + i)
        for j in range(i + 1, PAIRS):
            value = value - cross_gram[i][j] * coef_p[j]
        coef_p[i] = value / cross_gram[i][i]
    coef_q = [None] * PAIRS
    for i in range(PAIRS):
        value = cross_gram[i][i] * coef_p[i] - total(PRE + i)
        for j in range(PAIRS):
            value = value + curv_gram[i][j] * coef_p[j]
        for j in range(i):
            value = value - cross_gram[j][i] * coef_q[j]
        coef_q[i] = value / cross_gram[i][i]
    for c in range(3):
        value = first[c]
        for i in range(PAIRS):
            value = value + wide(coef_q[i]) * s_vec[i][c] - wide(coef_p[i]) * solved[i][c]
        out[c, 0] = -value

    for copy in started:
        copy.wait_send()
    pltpu.make_async_copy(rest_a, rest_a, a_send).wait()
    pltpu.make_async_copy(rest_b, rest_b, b_send).wait()


def per_device(partials, hist_s, hist_y):
    dma = pltpu.SemaphoreType.DMA
    f32 = jnp.float32
    chunk = (FIELDS, 8, 128)
    return pl.pallas_call(
        kernel,
        out_shape=jax.ShapeDtypeStruct((3, 1, 8, 128), f32),
        in_specs=[pl.BlockSpec(memory_space=pltpu.HBM)] * 3,
        out_specs=pl.BlockSpec(memory_space=pltpu.VMEM),
        scratch_shapes=[
            pltpu.VMEM((FIELDS, SHOT, 8, 128), f32),
            pltpu.VMEM((Z, *chunk), f32),
            pltpu.VMEM((6, *chunk), f32),
            pltpu.VMEM((6, *chunk), f32),
            pltpu.VMEM((PAIRS, 3, 8, 128), f32),
            pltpu.VMEM((PAIRS, 3, 8, 128), f32),
            pltpu.VMEM((2, 16, 128), f32),
            pltpu.VMEM((2, 16, 128), f32),
            pltpu.VMEM((8, 128), f32),
            pltpu.VMEM((6, 8, 128), f32),
            pltpu.VMEM((8, 128), f32),
            pltpu.VMEM((Z, 128), f32),
            pltpu.VMEM((8, 128), f32),
            pltpu.VMEM((X * GX * GY, 128), f32),
            pltpu.VMEM((SUMS, 128), f32),
            dma((3,)),
            dma((Z,)), dma((Z,)),
            dma((6,)), dma((6,)),
            dma((6,)), dma((6,)),
            dma((8,)), dma((8,)),
            dma, dma, dma, dma,
            pltpu.SemaphoreType.REGULAR((len(STEPS),)),
            pltpu.SemaphoreType.REGULAR((4,)),
        ],
        compiler_params=pltpu.CompilerParams(collective_id=0, has_side_effects=True, vmem_limit_bytes=56_512_000),
        name="lbfgs_direction",
    )(partials, hist_s, hist_y)


def solution(mesh):
    return jax.shard_map(
        per_device,
        mesh=mesh,
        in_specs=(
            P("shot", None, None, "gx", "gy"),
            P(None, None, "shot", "gx", "gy"),
            P(None, None, "shot", "gx", "gy"),
        ),
        out_specs=P(None, "shot", "gx", "gy"),
        check_vma=False,
    )
```

```python
import jax
import jax.numpy as jnp
from jax import lax
from jax.experimental import pallas as pl
from jax.experimental.pallas import tpu as pltpu
from jax.sharding import PartitionSpec as P

PAIRS = 5
FIELDS = 9
Z = 12
X = 2
SHOT = Z * X
GX = 4
GY = 8
MESH = pl.DeviceIdType.MESH
SPLIT = 5

ORDER = (6, 5, -5, 4, -4, 3, -3, 2, -2, 1, -1, 0)
STEPS = (1, 2, 3, -1, -2, -3)
LAST = {3: 0, -3: 1, 2: 2, -2: 3, 1: 4, -1: 5}

CROSS = 0
CURV = 32
HIST = 47
PRE = 52
SUMS = 64


def rows_of(terms):
    sub = lax.broadcasted_iota(jnp.int32, (8, 128), 0)
    out = jnp.zeros((8, 128), jnp.float32)
    for i, term in enumerate(terms):
        out = jnp.where(sub == i, jnp.sum(term, axis=0, keepdims=True), out)
    return jnp.broadcast_to(jnp.sum(out, axis=1, keepdims=True), (8, 128))


def row_of_sums(terms, first):
    sub = lax.broadcasted_iota(jnp.int32, (8, 128), 0)
    lane = lax.broadcasted_iota(jnp.int32, (8, 128), 1)
    total = jnp.zeros((8, 128), jnp.float32)
    for start in range(0, len(terms), 8):
        tile = rows_of(terms[start : start + 8])
        total = total + jnp.where(lane == sub + (first + start), tile, 0.0)
    return jnp.sum(total, axis=0, keepdims=True)


def dot_tile(left, right):
    return left[0] * right[0] + left[1] * right[1] + left[2] * right[2]


def kernel(
    partials, hist_s, hist_y, out,
    own, pair, stage, last, s_tile, y_tile,
    rows_out, rows_in, cols_out, cols_in,
    row_a, all_a, row_b, all_b, splat,
    local_sem, pair_send, pair_recv, stage_send, stage_recv, last_send, last_recv,
    halo_send, halo_recv, a_send, a_recv, b_send, b_recv, ready, known,
):
    shot = lax.axis_index("shot")
    gx = lax.axis_index("gx")
    gy = lax.axis_index("gy")
    z = lax.rem(shot, Z)
    xb = lax.div(shot, Z)
    base = xb * Z
    other = (1 - xb) * Z

    def along_z(step):
        return {"shot": base + lax.rem(z + (step + Z), Z)}

    def tile_peer(dx, dy):
        return {"gx": lax.rem(gx + (dx + GX), GX), "gy": lax.rem(gy + (dy + GY), GY)}

    far = lambda step, count: min(step, count - step)
    z_steps = sorted(range(1, Z), key=lambda dz: -far(dz, Z))
    plane_steps = [(dl, dx, dy) for dl in range(X) for dx in range(GX) for dy in range(GY)][1:]
    plane_steps.sort(key=lambda d: -(d[0] + far(d[1], GX) + far(d[2], GY)))

    def plane_peer(dl, dx, dy):
        return {"shot": (other if dl else base) + z} | tile_peer(dx, dy)

    local = [
        pltpu.make_async_copy(partials.at[0], own, local_sem.at[0]),
        pltpu.make_async_copy(hist_s.at[:, :, 0], s_tile, local_sem.at[1]),
        pltpu.make_async_copy(hist_y.at[:, :, 0], y_tile, local_sem.at[2]),
    ]
    for copy in local:
        copy.start()

    def plane(step):
        return lax.rem(z + (step + Z), Z)

    half = GY // 2
    ring = jnp.where(gy > half, GY - gy, gy)
    flip = {"gx": lax.rem(gx + 2, GX)}
    mate = {"gx": gx + 1 - 2 * lax.rem(gx, 2)}
    outer = [(tile_peer(0, 1), gy < half), (tile_peer(0, -1), (gy == 0) | (gy > half))]
    inner = [(tile_peer(0, -1), (gy > 0) & (gy <= half)), (tile_peer(0, 1), gy >= half)]
    barrier = pltpu.get_barrier_semaphore()

    def signal(sem, device):
        pl.semaphore_signal(sem, inc=1, device_id=device, device_id_type=MESH)

    def signal_if(wanted, sem, device):
        @pl.when(wanted)
        def _():
            signal(sem, device)

    signal(barrier, {"shot": other + z})
    signal(barrier, mate)
    expected = 2 + jnp.where(gx >= 2, 1, 0) + jnp.where(gy == half, 2, jnp.where(gy == 0, 0, 1))
    for device, wanted in outer:
        signal_if(wanted, barrier, device)
    signal_if(gx < 2, barrier, flip)
    for step in STEPS:
        signal_if(plane(step) > z, barrier, along_z(step))
        expected = expected + jnp.where(plane(step) < z, 1, 0)
    pl.semaphore_wait(barrier, expected)

    def tell_earlier():
        for step in STEPS:
            signal_if(plane(step) < z, ready.at[STEPS.index(-step)], along_z(step))
        signal_if(gx >= 2, known.at[0], flip)

    def await_plane(step):
        @pl.when(plane(step) > z)
        def _():
            pl.semaphore_wait(ready.at[STEPS.index(step)], 1)

    def know_row():
        @pl.when(gx < 2)
        def _():
            pl.semaphore_wait(known.at[0], 1)

        signal(known.at[1], mate)
        pl.semaphore_wait(known.at[1], 1)

        @pl.when(ring == half)
        def _():
            for device, _ in inner:
                signal(known.at[2], device)

    def know_outer(distance):
        @pl.when(ring == distance)
        def _():
            pl.semaphore_wait(known.at[2], 1 if distance else 2)
            if distance:
                for device, wanted in inner:
                    signal_if(wanted, known.at[2], device)
            else:
                for device, _ in outer:
                    signal(known.at[3], device)

    def know_all():
        @pl.when(ring > 0)
        def _():
            pl.semaphore_wait(known.at[3], jnp.where(ring == half, 2, 1))

            @pl.when(ring < half)
            def _():
                for device, wanted in outer:
                    signal_if(wanted, known.at[3], device)

    started = []

    def send(src, dst, send_sem, recv_sem, device):
        copy = pltpu.make_async_remote_copy(
            src_ref=src, dst_ref=dst, send_sem=send_sem, recv_sem=recv_sem, device_id=device, device_id_type=MESH
        )
        copy.start()
        started.append(copy)
        return copy

    local[0].wait()
    level = [lax.rem(z + (Z - s), Z) for s in ORDER]
    pair_copy = []
    for k in range(Z):
        pair_copy.append(
            send(own.at[:, other + level[k]], pair.at[k], pair_send.at[k], pair_recv.at[k], {"shot": other + z})
        )

    tell_earlier()
    local[1].wait()
    local[2].wait()
    s_vec = [[s_tile[i, c] for c in range(3)] for i in range(PAIRS)]
    y_vec = [[y_tile[i, c] for c in range(3)] for i in range(PAIRS)]
    cross = [dot_tile(s_vec[i], y_vec[j]) for i in range(PAIRS) for j in range(PAIRS)]
    row_a[0:1] = row_of_sums(cross, CROSS)

    know_row()
    slot = {s: k for k, s in enumerate(ORDER)}
    stage_copy = {}
    last_copy = {}
    for s in (6, 5, -5, 4, -4):
        k = slot[s]
        pair_copy[k].wait_recv()
        pair[k] = pair[k] + own[:, base + level[k]]
        if s == 5:
            know_outer(3)
        if s == 4:
            know_outer(2)
        if s == 6:
            await_plane(-3)
            await_plane(3)
            stage_copy["r6"] = send(
                pair.at[k, 0:SPLIT], stage.at[2, 0:SPLIT], stage_send.at[2], stage_recv.at[2], along_z(-3)
            )
            stage_copy["l6"] = send(
                pair.at[k, SPLIT:FIELDS], stage.at[5, SPLIT:FIELDS], stage_send.at[5], stage_recv.at[5], along_z(3)
            )
        elif s > 0:
            await_plane(3 - s)
            stage_copy[s] = send(pair.at[k], stage.at[s - 4], stage_send.at[s - 4], stage_recv.at[s - 4], along_z(3 - s))
        else:
            await_plane(-3 - s)
            stage_copy[s] = send(
                pair.at[k], stage.at[-s - 1], stage_send.at[-s - 1], stage_recv.at[-s - 1], along_z(-3 - s)
            )
    def add_own(s):
        k = slot[s]
        pair_copy[k].wait_recv()
        pair[k] = pair[k] + own[:, base + level[k]]

    def send_last(s):
        m = LAST[s]
        last_copy[s] = send(pair.at[slot[s]], last.at[m], last_send.at[m], last_recv.at[m], along_z(-s))

    def gather(s):
        k = slot[s]
        if s > 0:
            first_slot, low, high, far = 0, 0, SPLIT, "r6"
        else:
            first_slot, low, high, far = 3, SPLIT, FIELDS, "l6"
        add_own(s)
        for key in (far, s + s // 3 * 2, s + s // 3):
            stage_copy[key].wait_recv()
        pair[k] = pair[k] + stage[first_slot] + stage[first_slot + 1]
        pair[k, low:high] = pair[k, low:high] + stage[first_slot + 2, low:high]
        send_last(s)

    add_own(2)
    send_last(2)
    know_outer(1)
    add_own(-2)
    send_last(-2)
    gather(3)
    gather(-3)
    know_outer(0)
    add_own(1)
    send_last(1)
    add_own(-1)
    send_last(-1)
    know_all()
    k = slot[0]
    pair_copy[k].wait_recv()
    mine = pair[k] + own[:, shot]
    for s in (1, -1, 2, -2, 3, -3):
        last_copy[s].wait_recv()
        mine = mine + last[LAST[s]]
    mine = mine * (1.0 / SHOT)
    field = [mine[f] for f in range(FIELDS)]

    sub = lax.broadcasted_iota(jnp.int32, (8, 128), 0)
    lane = lax.broadcasted_iota(jnp.int32, (8, 128), 1)
    columns = jnp.zeros((8, 128), jnp.float32)
    for f in range(FIELDS):
        rows_out[0, f : f + 1] = field[f][0:1]
        rows_out[1, f : f + 1] = field[f][7:8]
        columns = jnp.where(lane == f, field[f] if f == 0 else pltpu.roll(field[f], f, 1), columns)
        columns = jnp.where(lane == 16 + f, pltpu.roll(field[f], 17 + f, 1), columns)
    cols_out[...] = columns
    halo = []
    for n, (dx, dy) in enumerate(((-1, -1), (1, -1), (-1, 1), (1, 1), (0, -1), (0, 1))):
        used = slice(7, 8) if dx > 0 else slice(0, 1) if dx < 0 else slice(0, 8)
        halo.append(send(cols_out.at[used], cols_in.at[n, used], halo_send.at[n], halo_recv.at[n], tile_peer(dx, dy)))
    halo.append(send(rows_out.at[0, 0:FIELDS], rows_in.at[0, 0:FIELDS], halo_send.at[6], halo_recv.at[6], tile_peer(-1, 0)))
    halo.append(send(rows_out.at[1, 0:FIELDS], rows_in.at[1, 0:FIELDS], halo_send.at[7], halo_recv.at[7], tile_peer(1, 0)))
    for copy in halo:
        copy.wait_recv()
    has_up, has_down = gx > 0, gx < GX - 1
    has_left, has_right = gy > 0, gy < GY - 1

    def along_x(center, above, below):
        up = jnp.where(sub == 0, jnp.where(has_up, above, 0.0), pltpu.roll(center, 1, 0))
        down = jnp.where(sub == 7, jnp.where(has_down, below, 0.0), pltpu.roll(center, 7, 0))
        return 0.25 * (up + 2.0 * center + down)

    def wide(row):
        return jnp.broadcast_to(row, (8, 128))

    left = along_x(cols_in[5], wide(cols_in[3, 7:8]), wide(cols_in[2, 0:1]))
    right = along_x(cols_in[4], wide(cols_in[1, 7:8]), wide(cols_in[0, 0:1]))
    left = jnp.where(has_left, left, 0.0)
    right = jnp.where(has_right, right, 0.0)
    smooth = []
    for f in range(FIELDS):
        mid = along_x(field[f], wide(rows_in[1, f : f + 1]), wide(rows_in[0, f : f + 1]))
        before = jnp.where(lane == 0, pltpu.roll(left, 112 - f, 1), pltpu.roll(mid, 1, 1))
        after = jnp.where(lane == 127, pltpu.roll(right, 127 - f, 1), pltpu.roll(mid, 127, 1))
        smooth.append(0.25 * (before + 2.0 * mid + after))

    gradient = smooth[0:3]
    diag_p, diag_s, diag_r, cross_ps, cross_pr, cross_sr = smooth[3:9]
    cof_pp = diag_s * diag_r - cross_sr * cross_sr
    cof_ps = cross_pr * cross_sr - cross_ps * diag_r
    cof_pr = cross_ps * cross_sr - diag_s * cross_pr
    cof_ss = diag_p * diag_r - cross_pr * cross_pr
    cof_sr = cross_ps * cross_pr - diag_p * cross_sr
    cof_rr = diag_p * diag_s - cross_ps * cross_ps
    inverse_det = 1.0 / (diag_p * cof_pp + cross_ps * cof_ps + cross_pr * cof_pr)

    def solve(v):
        return [
            (cof_pp * v[0] + cof_ps * v[1] + cof_pr * v[2]) * inverse_det,
            (cof_ps * v[0] + cof_ss * v[1] + cof_sr * v[2]) * inverse_det,
            (cof_pr * v[0] + cof_sr * v[1] + cof_rr * v[2]) * inverse_det,
        ]

    first = solve(gradient)
    solved = [solve(y_vec[i]) for i in range(PAIRS)]
    upper = [(i, j) for i in range(PAIRS) for j in range(i, PAIRS)]
    terms = [dot_tile(y_vec[i], solved[j]) for i, j in upper]
    terms += [dot_tile(s_vec[i], gradient) for i in range(PAIRS)]
    terms += [dot_tile(y_vec[i], first) for i in range(PAIRS)]
    row = row_a[0:1] + row_of_sums(terms, CURV)

    row_a[0:1] = row
    all_a[0:1] = row
    for n, dz in enumerate(z_steps):
        send(row_a.at[0:1], all_a.at[n + 1 : n + 2], a_send, a_recv, along_z(dz))
        started.pop()
    rest_a = all_a.at[1:Z]
    pltpu.make_async_copy(rest_a, rest_a, a_recv).wait()
    row = jnp.sum(all_a[...], axis=0, keepdims=True)
    row_b[0:1] = row
    all_b[0:1] = row
    for n, d in enumerate(plane_steps):
        send(row_b.at[0:1], all_b.at[n + 1 : n + 2], b_send, b_recv, plane_peer(*d))
        started.pop()
    rest_b = all_b.at[1 : X * GX * GY]
    for copy in started:
        copy.wait_send()
    pltpu.make_async_copy(rest_a, rest_a, a_send).wait()
    pltpu.make_async_copy(rest_b, rest_b, b_send).wait()
    pltpu.make_async_copy(rest_b, rest_b, b_recv).wait()
    row = jnp.sum(all_b[...], axis=0, keepdims=True)

    tall_row = lax.broadcasted_iota(jnp.int32, (SUMS, 128), 0)
    tall_lane = lax.broadcasted_iota(jnp.int32, (SUMS, 128), 1)
    picked = jnp.where(tall_row == tall_lane, jnp.broadcast_to(row, (SUMS, 128)), 0.0)
    splat[...] = jnp.broadcast_to(jnp.sum(picked, axis=1, keepdims=True), (SUMS, 128))

    def total(n):
        return splat[n : n + 1]

    cross_gram = [[total(CROSS + i * PAIRS + j) for j in range(PAIRS)] for i in range(PAIRS)]
    curv_gram = [[None] * PAIRS for _ in range(PAIRS)]
    for n, (i, j) in enumerate(upper):
        curv_gram[i][j] = curv_gram[j][i] = total(CURV + n)
    coef_p = [None] * PAIRS
    for i in range(PAIRS - 1, -1, -1):
        value = total(HIST + i)
        for j in range(i + 1, PAIRS):
            value = value - cross_gram[i][j] * coef_p[j]
        coef_p[i] = value / cross_gram[i][i]
    coef_q = [None] * PAIRS
    for i in range(PAIRS):
        value = cross_gram[i][i] * coef_p[i] - total(PRE + i)
        for j in range(PAIRS):
            value = value + curv_gram[i][j] * coef_p[j]
        for j in range(i):
            value = value - cross_gram[j][i] * coef_q[j]
        coef_q[i] = value / cross_gram[i][i]
    for c in range(3):
        value = first[c]
        for i in range(PAIRS):
            value = value + wide(coef_q[i]) * s_vec[i][c] - wide(coef_p[i]) * solved[i][c]
        out[c, 0] = -value


def per_device(partials, hist_s, hist_y):
    dma = pltpu.SemaphoreType.DMA
    f32 = jnp.float32
    chunk = (FIELDS, 8, 128)
    return pl.pallas_call(
        kernel,
        out_shape=jax.ShapeDtypeStruct((3, 1, 8, 128), f32),
        in_specs=[pl.BlockSpec(memory_space=pltpu.HBM)] * 3,
        out_specs=pl.BlockSpec(memory_space=pltpu.VMEM),
        scratch_shapes=[
            pltpu.VMEM((FIELDS, SHOT, 8, 128), f32),
            pltpu.VMEM((Z, *chunk), f32),
            pltpu.VMEM((6, *chunk), f32),
            pltpu.VMEM((6, *chunk), f32),
            pltpu.VMEM((PAIRS, 3, 8, 128), f32),
            pltpu.VMEM((PAIRS, 3, 8, 128), f32),
            pltpu.VMEM((2, 16, 128), f32),
            pltpu.VMEM((2, 16, 128), f32),
            pltpu.VMEM((8, 128), f32),
            pltpu.VMEM((6, 8, 128), f32),
            pltpu.VMEM((8, 128), f32),
            pltpu.VMEM((Z, 128), f32),
            pltpu.VMEM((8, 128), f32),
            pltpu.VMEM((X * GX * GY, 128), f32),
            pltpu.VMEM((SUMS, 128), f32),
            dma((3,)),
            dma((Z,)), dma((Z,)),
            dma((6,)), dma((6,)),
            dma((6,)), dma((6,)),
            dma((8,)), dma((8,)),
            dma, dma, dma, dma,
            pltpu.SemaphoreType.REGULAR((len(STEPS),)),
            pltpu.SemaphoreType.REGULAR((4,)),
        ],
        compiler_params=pltpu.CompilerParams(collective_id=0, has_side_effects=True, vmem_limit_bytes=56_512_000),
        name="lbfgs_direction",
    )(partials, hist_s, hist_y)


def solution(mesh):
    return jax.shard_map(
        per_device,
        mesh=mesh,
        in_specs=(
            P("shot", None, None, "gx", "gy"),
            P(None, None, "shot", "gx", "gy"),
            P(None, None, "shot", "gx", "gy"),
        ),
        out_specs=P(None, "shot", "gx", "gy"),
        check_vma=False,
    )
```
